32 devices in a mesh: seq: 8 (over z, y), dp: 4 (over x, core).
Axes of the slice: x: 2, y: 2, z: 4, core: 2. Of those that a mesh axis runs over, the one named last changes fastest.
Arguments:
- canvas_input: bfloat16 [12, 64, 32, 512], P('dp', 'seq'), may hold values from -6 to 6
- crop_heights: int32 [12, 4], P('dp'), may hold values from 1 to 61, as said below
- qkv_weight: bfloat16 [2, 512, 1536], P(None, ('seq', 'dp')), may hold values from -0.25 to 0.25
- merge_weight: bfloat16 [2, 512, 512], P(None, ('seq', 'dp')), may hold values from -2 to 2
- expand_weight: bfloat16 [2, 512, 2048], P(None, ('seq', 'dp')), may hold values from -0.25 to 0.25
- expand_bias: bfloat16 [2, 2048], P(None, ('seq', 'dp')), may hold values from -1.5 to 1.5
- reduce_weight: bfloat16 [2, 2048, 512], P(None, ('seq', 'dp')), may hold values from -0.25 to 0.25
- reduce_bias: bfloat16 [2, 512], P(None, ('seq', 'dp')), may hold values from -1.5 to 1.5
- norm_gain: bfloat16 [2, 2, 512], P(None, None, ('seq', 'dp')), may hold values from 0.3984375 to 1.59375
- norm_shift: bfloat16 [2, 2, 512], P(None, None, ('seq', 'dp')), may hold values from -1.5 to 1.5
- cotangent: bfloat16 [12, 64, 32, 512], P('dp', 'seq'), may hold values from -6 to 6
Outputs:
- block_output: bfloat16 [12, 64, 32, 512], P('dp', 'seq')
- input_grad: float32 [12, 64, 32, 512], P('dp', 'seq')
- qkv_grad: float32 [2, 512, 1536], P(None, ('seq', 'dp'))
- merge_grad: float32 [2, 512, 512], P(None, ('seq', 'dp'))
- expand_grad: float32 [2, 512, 2048], P(None, ('seq', 'dp'))
- expand_bias_grad: float32 [2, 2048], P(None, ('seq', 'dp'))
- reduce_grad: float32 [2, 2048, 512], P(None, ('seq', 'dp'))
- reduce_bias_grad: float32 [2, 512], P(None, ('seq', 'dp'))
- gain_grad: float32 [2, 2, 512], P(None, None, ('seq', 'dp'))
- shift_grad: float32 [2, 2, 512], P(None, None, ('seq', 'dp'))
The draws below stay inside these ranges and needn't reach their ends.
Inputs may be any that keep to these rules, and one draw needn't show every extreme that they name: `crop_heights`: each canvas's 4 crop heights are at least 1 and sum to 64. In every index of dp one of its 3 canvases, which one drawn from the seed, has a first crop of 61 rows and three more of one row.
All inputs are finite; a program needn't handle non-finite values.
Results may differ from the reference program's by a relative error of at most 0.025.
Values may be sent and summed in bfloat16 or wider, within the bound.
No kernel may reach another device: no remote copies, remote signals or barrier semaphores. Data moves between devices by JAX's collectives and lax.ppermute only.
A program may use at most 192 MiB of HBM per device.

```python
import jax
import jax.numpy as jnp
from jax import lax

D = 512
HEADS = 8
HEAD_DIM = 64
FF = 2048
LAYERS = 2
MICRO = 3
BAND = 8
QW = 32
COLS = 32
NCROP = 4
ROWS = 64
CANVASES = 12


def draw_crop_heights(key, part):
    key = jax.random.fold_in(key, 11)
    pick_key, cut_key = jax.random.split(key)
    groups = CANVASES // MICRO
    chosen = jax.random.randint(pick_key, (groups,), 0, MICRO)
    canvas_keys = jax.random.split(cut_key, CANVASES)

    def one_canvas(canvas_key):
        cuts = jnp.sort(jax.random.permutation(canvas_key, ROWS - 1)[:NCROP - 1] + 1).astype(jnp.int32)
        bounds = jnp.concatenate([jnp.zeros((1,), jnp.int32), cuts, jnp.full((1,), ROWS, jnp.int32)])
        return bounds[1:] - bounds[:-1]
    random_heights = jax.vmap(one_canvas)(canvas_keys)
    long_crop = jnp.concatenate([jnp.full((1,), ROWS - NCROP + 1, jnp.int32), jnp.ones((NCROP - 1,), jnp.int32)])
    canvas_index = jnp.arange(CANVASES)
    special = canvas_index % MICRO == chosen[canvas_index // MICRO]
    return jnp.where(special[:, None], long_crop[None, :], random_heights).astype(jnp.int32)


def block_scale(rng, dims, shards, least, top_value):
    factor_of = 1.0
    for axis_at, shards_of in shards:
        draws = jax.random.uniform(jax.random.fold_in(jax.random.fold_in(rng, 6), axis_at), (shards_of,), jnp.float32, least / len(shards), top_value / len(shards))
        factor_of = factor_of * jnp.repeat(jnp.exp(draws), dims[axis_at] // shards_of).reshape((-1,) + (1,) * (len(dims) - 1 - axis_at))
    return factor_of


def gaussian(key, extent, spread, most, cuts=(), kind=jnp.bfloat16):
    values = jax.random.normal(key, extent, jnp.float32) * spread
    if len(cuts) > 0:
        values = block_scale(key, extent, cuts, -0.22, 0.18) * values
    return jnp.clip(values, min=-most, max=most).astype(kind)


def setup_inputs(seed: int = 0) -> dict:
    key_list = jax.random.split(jax.random.key(seed), 12)
    return {
        "canvas_input": gaussian(key_list[0], (CANVASES, ROWS, COLS, D), 1.0, 6.0, ((0, 4), (1, 8))),
        "crop_heights": draw_crop_heights(jax.random.fold_in(key_list[11], 71), 0),
        "qkv_weight": gaussian(key_list[2], (LAYERS, D, 3 * D), D ** -0.5, 0.25, ((1, 32),)),
        "merge_weight": gaussian(key_list[3], (LAYERS, D, D), (D // 64) ** -0.5, 2.0, ((1, 32),)),
        "expand_weight": gaussian(key_list[4], (LAYERS, D, FF), D ** -0.5, 0.25, ((1, 32),)),
        "expand_bias": gaussian(key_list[5], (LAYERS, FF), 0.3, 1.5, ((1, 32),)),
        "reduce_weight": gaussian(key_list[6], (LAYERS, FF, D), (FF // 4) ** -0.5, 0.25, ((1, 32),)),
        "reduce_bias": gaussian(key_list[7], (LAYERS, D), 0.3, 1.5, ((1, 32),)),
        "norm_gain": jnp.clip(1.0 + 0.12 * jax.random.normal(key_list[8], (LAYERS, 2, D), jnp.float32), 0.3984375, 1.59375).astype(jnp.bfloat16),
        "norm_shift": gaussian(key_list[9], (LAYERS, 2, D), 0.3, 1.5, ((2, 32),)),
        "cotangent": gaussian(key_list[10], (CANVASES, ROWS, COLS, D), 1.0, 6.0, ((0, 4), (1, 8))),
    }


epsilon = 1e-05
masked_score = -1e+30
highest = lax.Precision.HIGHEST

@jax.custom_vjp
def low(v):
    return lax.optimization_barrier(v.astype(jnp.bfloat16)).astype(jnp.float32)

@jax.custom_vjp
def low_back(v):
    return v

def low_keep(v):
    return (low(v), None)

def low_pass(kept, grad):
    return (grad,)

def back_keep(v):
    return (v, None)

def back_low(kept, grad):
    return (low(grad),)
low.defvjp(low_keep, low_pass)
low_back.defvjp(back_keep, back_low)

def gelu_tanh(values):
    return 0.5 * values * (1.0 + jnp.tanh(0.7978845608028654 * (values + 0.044715 * values * values * values)))

def layer_norm(values, gain, shift):
    average = lax.optimization_barrier(jnp.mean(values, axis=-1, keepdims=True))
    centred = values - average
    variance = lax.optimization_barrier(jnp.mean(centred * centred, axis=-1, keepdims=True))
    return centred * lax.rsqrt(variance + epsilon) * gain + shift

def band_mask(first_row, crop_query, crop_key):
    query_pos = jnp.arange(BAND * COLS, dtype=jnp.int32)
    key_pos = jnp.arange(2 * BAND * COLS, dtype=jnp.int32)
    query_row = first_row + query_pos // COLS
    query_col = query_pos % COLS
    key_row = first_row - BAND + key_pos // COLS
    key_col = key_pos % COLS
    start = query_col // QW * QW - QW // 2
    earlier = (key_row[None, :] < query_row[:, None]) | (key_row[None, :] == query_row[:, None]) & (key_col[None, :] <= query_col[:, None])
    window = (key_col[None, :] >= start[:, None]) & (key_col[None, :] < start[:, None] + 2 * QW)
    return earlier & window & (key_row[None, :] >= 0) & (crop_key[None, :] == crop_query[:, None])

def product(left, right):
    return jnp.dot(left, right, precision=highest, preferred_element_type=jnp.float32)

def band_attend(items):
    queries, pair, first_row, crop_query, crop_key = items
    keys_band = pair[:, :D].reshape(2 * BAND * COLS, HEADS, HEAD_DIM)
    values = pair[:, D:].reshape(2 * BAND * COLS, HEADS, HEAD_DIM)
    scores = low_back(jnp.einsum('qhd,khd->hqk', queries, keys_band, precision=highest) * HEAD_DIM ** (-0.5))
    masked = jnp.where(band_mask(first_row, crop_query, crop_key)[None], scores, masked_score)
    largest = lax.optimization_barrier(jnp.max(masked, axis=-1, keepdims=True))
    powers = jnp.exp(masked - largest)
    soft = powers / lax.optimization_barrier(jnp.sum(powers, axis=-1, keepdims=True))
    return jnp.einsum('hqk,khd->qhd', low(soft), values, precision=highest)

def image_block(hidden, crop_row, params):
    qkv_weight, merge_weight, expand_weight, expand_bias, reduce_weight, reduce_bias, norm_gain, norm_shift = params
    bands = ROWS // BAND
    span = BAND * COLS
    packed = low_back(low(product(low(hidden), qkv_weight)))
    queries = packed[:, :D].reshape(bands, span, HEADS, HEAD_DIM)
    own_pair = packed[:, D:].reshape(bands, span, 2 * D)
    before_pair = jnp.concatenate([jnp.zeros((1, span, 2 * D), jnp.float32), own_pair[:-1]], axis=0)
    pair_all = jnp.concatenate([before_pair, own_pair], axis=1)
    crop_own = jnp.repeat(crop_row, COLS).reshape(bands, span)
    crop_before = jnp.concatenate([jnp.zeros((1, span), jnp.int32), crop_own[:-1]], axis=0)
    crop_key = jnp.concatenate([crop_before, crop_own], axis=1)
    first_rows = jnp.arange(bands, dtype=jnp.int32) * BAND
    attended = lax.map(jax.checkpoint(band_attend), (queries, pair_all, first_rows, crop_own, crop_key))
    attended = low_back(low(attended.reshape(ROWS * COLS, D)))
    first_in = hidden + low_back(product(attended, merge_weight))
    normed = layer_norm(first_in, norm_gain[0], norm_shift[0])
    inner_units = low_back(product(low(normed), expand_weight) + expand_bias)
    lifted = low(gelu_tanh(inner_units))
    output = low_back(product(lifted, reduce_weight) + reduce_bias)
    return layer_norm(normed + output, norm_gain[1], norm_shift[1])

def reference(canvas_input, crop_heights, qkv_weight, merge_weight, expand_weight, expand_bias, reduce_weight, reduce_bias, norm_gain, norm_shift, cotangent):
    weights = jax.tree.map(lambda weight: weight.astype(jnp.float32), (qkv_weight, merge_weight, expand_weight, expand_bias, reduce_weight, reduce_bias, norm_gain, norm_shift))
    pictures = canvas_input.astype(jnp.float32)
    crop_ends = jnp.cumsum(crop_heights, axis=1).astype(jnp.int32)
    row_index = jnp.arange(ROWS, dtype=jnp.int32)
    crop_rows = lax.optimization_barrier(jnp.sum((row_index[None, :, None] >= crop_ends[:, None, :]).astype(jnp.int32), axis=2)).astype(jnp.int32)

    def forward(canvases, layer_weights):

        def one_canvas(items):
            picture, crop_row = items
            hidden = picture.reshape(ROWS * COLS, D)
            for layer_index in range(LAYERS):
                hidden = image_block(hidden, crop_row, jax.tree.map(lambda weight: weight[layer_index], layer_weights))
            return hidden.reshape(ROWS, COLS, D)
        return lax.map(one_canvas, (canvases, crop_rows))
    result, pullback = jax.vjp(forward, pictures, weights)
    input_grad, weight_grads = pullback(cotangent.astype(jnp.float32))
    qkv_grad, merge_grad, expand_grad, expand_bias_grad, reduce_grad, reduce_bias_grad, gain_grad, shift_grad = weight_grads
    return (result.astype(jnp.bfloat16), input_grad, qkv_grad, merge_grad, expand_grad, expand_bias_grad, reduce_grad, reduce_bias_grad, gain_grad, shift_grad)
```

```python
import functools

import jax
import jax.numpy as jnp
from jax import lax
from jax.experimental import pallas as pl
from jax.experimental.pallas import tpu as pltpu
from jax.sharding import PartitionSpec as P

D = 512
HEADS = 8
HEAD_DIM = 64
FF = 2048
LAYERS = 2
BAND = 8
QW = 32
COLS = 32
SPAN = BAND * COLS

F32 = jnp.float32
BF16 = jnp.bfloat16
epsilon = 1e-05
masked_score = -1e30
VMEM_BYTES = 60 * 1024 * 1024
SMALL = 256


def dot(left, right, left_axis, right_axis):
    return lax.dot_general(
        left, right, (((left_axis,), (right_axis,)), ((), ())), preferred_element_type=F32
    )


class Layout:
    def __init__(self, seq, dp):
        self.seq, self.dp = seq, dp
        self.devices = seq * dp
        self.rows = D // self.devices
        self.far = seq // 2
        self.direct = self.rows % 16 == 0
        bits = []
        bit = seq // 2
        while bit > 1:
            bits.append(bit)
            bit //= 2
        self.far_bits = bits
        codes = [0]
        for bit in bits:
            codes = codes + [c ^ bit for c in codes]
        self.far_codes = codes

    def place(self, code):
        seq_code = code // self.dp
        at = seq_code * 0
        for step, bit in enumerate(self.far_bits):
            at = at + ((seq_code // bit) % 2) * (1 << step)
        quadrant = ((code // 2) % 2) + 2 * (seq_code % 2)
        return at + self.far * quadrant + 4 * self.far * (code % 2)

    def codes(self):
        order = [0] * self.devices
        for code in range(self.devices):
            order[self.place(code)] = code
        return order


def exchange(block, axis, size, bit):
    return lax.ppermute(block, axis, [(i, i ^ bit) for i in range(size)])


def gather_blocks(shard, layout):
    blocks = shard[None]
    for bit in layout.far_bits:
        other = exchange(blocks, "seq", layout.seq, bit)
        blocks = jnp.concatenate([blocks, other], axis=0)
    far = [c * layout.dp for c in layout.far_codes]
    half = layout.far // 2
    x_bit, y_bit = 2, layout.dp
    by_x = exchange(blocks, "dp", layout.dp, 2)
    by_y = exchange(blocks, "seq", layout.seq, 1)
    diagonal_x = exchange(by_y[:half], "dp", layout.dp, 2)
    diagonal_y = exchange(by_x[half:], "seq", layout.seq, 1)
    held = [
        (blocks, far),
        (by_x, [c ^ x_bit for c in far]),
        (by_y, [c ^ y_bit for c in far]),
        (diagonal_x, [c ^ x_bit ^ y_bit for c in far[:half]]),
        (diagonal_y, [c ^ x_bit ^ y_bit for c in far[half:]]),
    ]
    return held + [
        (exchange(array, "dp", layout.dp, 1), [c ^ 1 for c in codes]) for array, codes in held
    ]


def gathered(shard, layout, me):
    held = gather_blocks(shard, layout)
    if layout.direct:
        return tuple(a for a, _ in held), tuple(tuple(c) for _, c in held)
    every = jnp.concatenate([a for a, _ in held], axis=0)
    codes = sum((list(c) for _, c in held), [])
    place_of = [0] * layout.devices
    for at, code in enumerate(codes):
        place_of[code] = at
    order = jnp.asarray(place_of, jnp.int32)[me ^ jnp.arange(layout.devices, dtype=jnp.int32)]
    whole = jnp.take(every, order, axis=0).reshape(1, D, shard.shape[1])
    return (whole,), ((0,),)


def add_low(left, right):
    return (left.astype(F32) + right.astype(F32)).astype(BF16)


def scatter_sum(keep, send, layout):
    far, half = layout.far, layout.far // 2
    total = add_low(keep, exchange(send, "dp", layout.dp, 1))
    own, to_x, to_y, diagonal = (total[far * i : far * (i + 1)] for i in range(4))
    from_x = exchange(diagonal[:half], "dp", layout.dp, 2)
    from_y = exchange(diagonal[half:], "seq", layout.seq, 1)
    to_x = jnp.concatenate([to_x[:half], add_low(to_x[half:], from_y)], axis=0)
    to_y = jnp.concatenate([add_low(to_y[:half], from_x), to_y[half:]], axis=0)
    by_x = exchange(to_x, "dp", layout.dp, 2)
    by_y = exchange(to_y, "seq", layout.seq, 1)
    total = own.astype(F32) + by_x.astype(F32) + by_y.astype(F32)
    for bit in layout.far_bits[::-1]:
        half = total.shape[0] // 2
        other = exchange(total[half:].astype(BF16), "seq", layout.seq, bit)
        total = total[:half] + other.astype(F32)
    return total[0]


def split_blocks(arrays, layout, me):
    if layout.direct:
        return arrays
    blocks = arrays[0].reshape(layout.devices, layout.rows, arrays[0].shape[2])
    order = me ^ jnp.asarray(layout.codes(), jnp.int32)
    blocks = jnp.take(blocks, order, axis=0)
    half = layout.devices // 2
    return blocks[:half], blocks[half:]


def block_copies(me, rows, buffers, codes, lane, width, target, sems):
    copies = []
    for buffer, buffer_codes in zip(buffers, codes):
        for at, code in enumerate(buffer_codes):
            row = pl.multiple_of((me ^ code) * rows, rows)
            copies.append(
                pltpu.make_async_copy(
                    buffer.at[at, :, pl.ds(lane, width)],
                    target.at[pl.ds(row, rows), :],
                    sems.at[len(copies)],
                )
            )
    return copies


def small_parts(rows):
    return [
        (0, 4 * rows),
        (4 * rows, rows),
        (5 * rows, rows),
        (6 * rows, rows),
        (7 * rows, rows),
        (8 * rows, rows),
    ]


def row_pick(devices, rows, row):
    device = lax.broadcasted_iota(jnp.int32, (devices, devices * rows), 0)
    at = lax.broadcasted_iota(jnp.int32, (devices, devices * rows), 1)
    return (at == device * rows + row).astype(BF16)


def lane_pick(offset, width, length):
    lane = lax.broadcasted_iota(jnp.int32, (SMALL, length), 0)
    at = lax.broadcasted_iota(jnp.int32, (SMALL, length), 1)
    return (lane - offset == jnp.bitwise_and(at, width - 1)).astype(BF16)


def unpack_small(small, table, layout):
    devices, rows = layout.devices, layout.rows
    for layer in range(LAYERS):
        lanes = dot(row_pick(devices, rows, layer), small[...], 1, 0).astype(BF16)
        for index, (offset, width) in enumerate(small_parts(rows)):
            length = devices * width
            spread = dot(lanes, lane_pick(offset, width, length), 1, 0)
            device = lax.broadcasted_iota(jnp.int32, (devices, length), 0)
            at = lax.broadcasted_iota(jnp.int32, (devices, length), 1)
            mine = device == lax.shift_right_logical(at, width.bit_length() - 1)
            values = jnp.sum(jnp.where(mine, spread, 0.0), axis=0, keepdims=True)
            table[pl.ds(6 * layer + index, 1), pl.ds(0, length)] = values


def pack_small(me, vectors, layout):
    devices, rows = layout.devices, layout.rows
    lanes = jnp.zeros((devices, SMALL), F32)
    for vector, (offset, width) in zip(vectors, small_parts(rows)):
        length = devices * width
        at = lax.broadcasted_iota(jnp.int32, (1, length), 1)
        code = jnp.bitwise_xor(lax.shift_right_logical(at, width.bit_length() - 1), me)
        place = layout.place(code) if layout.direct else code
        row = lax.broadcasted_iota(jnp.int32, (devices, length), 0)
        spread = jnp.where(row == place, vector, 0.0).astype(BF16)
        lanes = lanes + dot(spread, lane_pick(offset, width, length), 1, 1)
    return dot(row_pick(devices, rows, 0), lanes.astype(BF16), 0, 0).astype(BF16)


def store_blocks(me, values, targets, lane, layout, first=0, rows=None):
    rows = layout.rows if rows is None else rows
    width = values.shape[1]
    if not layout.direct:
        targets[0][0, pl.ds(first * rows, values.shape[0]), pl.ds(lane, width)] = values
        return
    half = layout.devices // 2
    for index in range(values.shape[0] // rows):
        part = values[index * rows : (index + 1) * rows, :]
        place = layout.place(jnp.bitwise_xor(first + index, me))

        @pl.when(place < half)
        def _():
            targets[0][place, :, pl.ds(lane, width)] = part

        @pl.when(place >= half)
        def _():
            targets[1][place - half, :, pl.ds(lane, width)] = part


def allowed_bias(info, canvas, crops):
    first_row = info[1]
    key = lax.broadcasted_iota(jnp.int32, (2 * SPAN, SPAN), 0)
    query = lax.broadcasted_iota(jnp.int32, (2 * SPAN, SPAN), 1)
    key_row = first_row - BAND + key // COLS
    query_row = first_row + query // COLS
    key_col, query_col = key % COLS, query % COLS
    key_label = jnp.zeros_like(key)
    query_label = jnp.zeros_like(query)
    end = 0
    for crop in range(crops):
        end = end + info[2 + canvas * crops + crop]
        key_label = key_label + (key_row >= end).astype(jnp.int32)
        query_label = query_label + (query_row >= end).astype(jnp.int32)
    start = query_col // QW * QW - QW // 2
    allowed = (key - SPAN <= query) & (key_row >= 0) & (key_label == query_label)
    allowed = allowed & (key_col >= start) & (key_col < start + 2 * QW)
    return jnp.where(allowed, 0.0, masked_score).astype(F32)


def normalised(values):
    centred = values - jnp.mean(values, axis=-1, keepdims=True)
    variance = jnp.mean(centred * centred, axis=-1, keepdims=True)
    scale = lax.rsqrt(variance + epsilon)
    return centred * scale, scale


def norm_back(grad, values, gain):
    hat, scale = normalised(values)
    scaled = grad * gain
    mean_one = jnp.mean(scaled, axis=-1, keepdims=True)
    mean_two = jnp.mean(scaled * hat, axis=-1, keepdims=True)
    return (
        scale * (scaled - mean_one - hat * mean_two),
        jnp.sum(grad * hat, axis=0, keepdims=True),
        jnp.sum(grad, axis=0, keepdims=True),
        hat,
    )


def attend_kernel(layout, codes, crops, first_layer, info, hidden, flank, *refs):
    count = len(codes)
    buffers, refs = refs[:count], refs[count:]
    if first_layer:
        qkv, merge, table, queries, keys, values, soft, attended, first_in, small, sems = refs
    else:
        qkv, merge, queries, keys, values, soft, attended, first_in, sems = refs
    canvas = pl.program_id(0)
    me = info[0]
    rows = layout.rows if layout.direct else D

    @pl.when(canvas == 0)
    def _():
        copies = block_copies(me, rows, buffers, codes, 0, 3 * D, qkv, sems.at[0])
        copies += block_copies(me, rows, buffers, codes, 3 * D, D, merge, sems.at[1])
        if first_layer:
            copies += block_copies(me, rows, buffers, codes, 4 * D, SMALL, small, sems.at[2])
        for copy in copies:
            copy.start()
        for copy in copies:
            copy.wait()
        if first_layer:
            unpack_small(small, table, layout)

    bias = allowed_bias(info, canvas, crops)
    own = hidden[...].astype(F32)
    own_low = hidden[...].astype(BF16)
    packed = jnp.transpose(dot(own_low, qkv[...], 1, 0))
    before = jnp.transpose(dot(flank[...], qkv[:, D:], 1, 0))
    queries[0] = packed[:D].astype(BF16) * HEAD_DIM ** (-0.5)
    keys[0, :, :SPAN] = before[:D].astype(BF16)
    keys[0, :, SPAN:] = packed[D : 2 * D].astype(BF16)
    values[0, :, :SPAN] = before[D:].astype(BF16)
    values[0, :, SPAN:] = packed[2 * D :].astype(BF16)
    for head in range(HEADS):
        at = pl.ds(head * HEAD_DIM, HEAD_DIM)
        scores = dot(keys[0, at, :], queries[0, at, :], 0, 0) + bias
        largest = jnp.max(scores, axis=0, keepdims=True)
        powers = jnp.exp(scores - largest)
        total = jnp.sum(powers, axis=0, keepdims=True)
        low = (powers * (1.0 / total)).astype(BF16)
        soft[0, head] = low
        attended[at, :] = dot(values[0, at, :], low, 1, 0).astype(BF16)
    first_in[...] = own + dot(attended[...], merge[...], 0, 0)


def attend(layout, first_layer, info, hidden, flank, buffers, codes, crops):
    tokens = hidden.shape[0]
    canvases = tokens // SPAN
    const = lambda shape: pl.BlockSpec(shape, lambda c: (0,) * len(shape))
    by_canvas = lambda *shape: pl.BlockSpec((1,) + shape, lambda c: (c,) + (0,) * len(shape))
    rows = pl.BlockSpec((SPAN, D), lambda c: (c, 0))
    outs = [((D, 3 * D), BF16, const((D, 3 * D))), ((D, D), BF16, const((D, D)))]
    if first_layer:
        outs.append(((16, FF), F32, const((16, FF))))
    outs += [
        ((canvases, D, SPAN), BF16, by_canvas(D, SPAN)),
        ((canvases, D, 2 * SPAN), BF16, by_canvas(D, 2 * SPAN)),
        ((canvases, D, 2 * SPAN), BF16, by_canvas(D, 2 * SPAN)),
        ((canvases, HEADS, 2 * SPAN, SPAN), BF16, by_canvas(HEADS, 2 * SPAN, SPAN)),
        ((D, tokens), BF16, pl.BlockSpec((D, SPAN), lambda c: (0, c))),
        ((tokens, D), F32, rows),
    ]
    blocks = sum(len(c) for c in codes)
    scratch = [pltpu.VMEM((D, SMALL), BF16)] if first_layer else []
    return pl.pallas_call(
        functools.partial(attend_kernel, layout, codes, crops, first_layer),
        grid=(canvases,),
        in_specs=[pl.BlockSpec(memory_space=pltpu.SMEM), rows, rows]
        + [pl.BlockSpec(memory_space=pl.ANY)] * len(buffers),
        out_specs=[spec for _, _, spec in outs],
        out_shape=[jax.ShapeDtypeStruct(shape, kind) for shape, kind, _ in outs],
        scratch_shapes=scratch + [pltpu.SemaphoreType.DMA((3, blocks))],
        compiler_params=pltpu.CompilerParams(vmem_limit_bytes=VMEM_BYTES),
        cost_estimate=pl.CostEstimate(
            flops=tokens * D * D * 2 * 20, bytes_accessed=20 << 20, transcendentals=0
        ),
        name="attend",
    )(info, hidden, flank, *buffers)


def feed_kernel(layout, codes, layer, lane, info, table, first_in, *refs):
    count = len(codes)
    buffers, refs = refs[:count], refs[count:]
    expand, reduce, second_in, lifted, slope, result, result_low, folded, sems = refs
    me = info[0]
    rows = layout.rows if layout.direct else D
    shard = layout.rows

    @pl.when(pl.program_id(0) == 0)
    def _():
        copies = block_copies(me, rows, buffers, codes, lane, FF, expand, sems.at[0])
        copies += block_copies(me, rows, buffers, codes, lane + FF, FF, folded, sems.at[1])
        for copy in copies:
            copy.start()
        for copy in copies:
            copy.wait()
        for device in range(layout.devices):
            for part in range(4):
                reduce[pl.ds((device * 4 + part) * shard, shard), :] = folded[
                    pl.ds(device * shard, shard), pl.ds(part * D, D)
                ]

    row = lambda index, width: table[pl.ds(6 * layer + index, 1), pl.ds(0, width)]
    normed = normalised(first_in[...])[0] * row(2, D) + row(4, D)
    inner = dot(normed.astype(BF16), expand[...], 1, 0) + row(0, FF)
    square = inner * inner
    bend = jnp.tanh(0.7978845608028654 * (inner + 0.044715 * square * inner))
    rising = 0.5 * (1.0 + bend)
    low = (inner * rising).astype(BF16)
    lifted[...] = low
    slope[...] = (
        rising
        + 0.5
        * inner
        * (1.0 - bend * bend)
        * (0.7978845608028654 + 3.0 * 0.044715 * 0.7978845608028654 * square)
    ).astype(BF16)
    second = normed + (dot(low, reduce[...], 1, 0) + row(1, D))
    second_in[...] = second
    out = normalised(second)[0] * row(3, D) + row(5, D)
    result[...] = out
    result_low[...] = out.astype(BF16)


def feed(layout, layer, info, table, first_in, buffers, codes, lane):
    tokens = first_in.shape[0]
    const = lambda *shape: pl.BlockSpec(shape, lambda c: (0,) * len(shape))
    rows = lambda width: pl.BlockSpec((SPAN, width), lambda c: (c, 0))
    outs = [
        ((D, FF), BF16, const(D, FF)),
        ((FF, D), BF16, const(FF, D)),
        ((tokens, D), F32, rows(D)),
        ((tokens, FF), BF16, rows(FF)),
        ((tokens, FF), BF16, rows(FF)),
        ((tokens, D), F32, rows(D)),
        ((tokens, D), BF16, rows(D)),
    ]
    blocks = sum(len(c) for c in codes)
    return pl.pallas_call(
        functools.partial(feed_kernel, layout, codes, layer, lane),
        grid=(tokens // SPAN,),
        in_specs=[pl.BlockSpec(memory_space=pltpu.SMEM), const(16, FF), rows(D)]
        + [pl.BlockSpec(memory_space=pl.ANY)] * len(buffers),
        out_specs=[spec for _, _, spec in outs],
        out_shape=[jax.ShapeDtypeStruct(shape, kind) for shape, kind, _ in outs],
        scratch_shapes=[pltpu.VMEM((D, FF), BF16), pltpu.SemaphoreType.DMA((2, blocks))],
        compiler_params=pltpu.CompilerParams(vmem_limit_bytes=VMEM_BYTES),
        cost_estimate=pl.CostEstimate(
            flops=tokens * D * FF * 4, bytes_accessed=20 << 20, transcendentals=0
        ),
        name="feed",
    )(info, table, first_in, *buffers)


def feed_back_kernel(layout, layer, returned, info, table, *refs):
    if returned:
        grad, back, second_in, first_in, lifted, slope, expand, reduce, *refs = refs
    else:
        grad, second_in, first_in, lifted, slope, expand, reduce, *refs = refs
    g_first, *targets = refs[: -5]
    g_out, normed_low, g_normed, vectors, bias_grad = refs[-5:]
    chunk = pl.program_id(0)
    chunks = pl.num_programs(0)
    me = info[0]
    width = expand.shape[1]
    tokens = g_first.shape[0]
    row = lambda index, size: table[pl.ds(6 * layer + index, 1), pl.ds(0, size)]

    @pl.when(chunk == 0)
    def _():
        vectors[...] = jnp.zeros_like(vectors)
        for part in range(tokens // SPAN):
            at = pl.ds(part * SPAN, SPAN)
            above = grad[at, :].astype(F32)
            if returned:
                above = above + back[at, :].astype(F32)
            g_second, gain, shift, _ = norm_back(above, second_in[at, :], row(3, D))
            low = g_second.astype(BF16)
            g_out[at, :] = low
            g_normed[at, :] = g_second
            normed_low[at, :] = (
                normalised(first_in[at, :])[0] * row(2, D) + row(4, D)
            ).astype(BF16)
            vectors[1:2, :] += jnp.sum(low.astype(F32), axis=0, keepdims=True)
            vectors[3:4, :] += gain
            vectors[5:6, :] += shift

    g_lifted = dot(g_out[...], reduce[...], 1, 1)
    g_inner = g_lifted * slope[...].astype(F32)
    low = g_inner.astype(BF16)
    bias_grad[:, pl.ds(pl.multiple_of(chunk * width, width), width)] = jnp.sum(
        low.astype(F32), axis=0, keepdims=True
    )
    reduce_grad = dot(lifted[...], g_out[...], 0, 0).astype(BF16)
    shard = layout.rows
    if layout.direct:
        per = width // (4 * shard)
        half = layout.devices // 2
        for index in range(per):
            place = layout.place(jnp.bitwise_xor(chunk * per + index, me))
            for part in range(4):
                at = (index * 4 + part) * shard
                piece = reduce_grad[at : at + shard, :]
                lanes = pl.ds(FF + part * D, D)

                @pl.when(place < half)
                def _():
                    targets[0][place, :, lanes] = piece

                @pl.when(place >= half)
                def _():
                    targets[1][place - half, :, lanes] = piece
    else:
        targets[1][pl.ds(pl.multiple_of(chunk * width, width), width), :] = reduce_grad
    expand_grad = dot(normed_low[...], low, 0, 0).astype(BF16)
    store_blocks(me, expand_grad, targets, pl.multiple_of(chunk * width, width), layout)
    g_normed[...] += dot(low, expand[...], 1, 1)

    @pl.when(chunk == chunks - 1)
    def _():
        for part in range(tokens // SPAN):
            at = pl.ds(part * SPAN, SPAN)
            below, gain, shift, _ = norm_back(g_normed[at, :], first_in[at, :], row(2, D))
            g_first[at, :] = below
            vectors[2:3, :] += gain
            vectors[4:5, :] += shift
        small = [bias_grad[...]] + [vectors[i : i + 1, :] for i in range(1, 6)]
        packed = pack_small(me, small, layout)
        if layout.direct:
            half = layout.devices // 2
            blocks = packed.reshape(layout.devices, layout.rows, SMALL)
            targets[0][:, :, 2 * FF :] = blocks[:half]
            targets[1][:, :, 2 * FF :] = blocks[half:]
        else:
            targets[0][0, :, FF:] = packed


def feed_back(layout, layer, info, table, grad, back, second_in, first_in, lifted, slope, expand, reduce):
    tokens = first_in.shape[0]
    width = 512
    chunks = FF // width
    const = lambda *shape: pl.BlockSpec(shape, lambda c: (0,) * len(shape))
    ins = [(grad, const(tokens, D))]
    if back is not None:
        ins.append((back, const(tokens, D)))
    ins += [
        (second_in, const(tokens, D)),
        (first_in, const(tokens, D)),
        (lifted, pl.BlockSpec((tokens, width), lambda c: (0, c))),
        (slope, pl.BlockSpec((tokens, width), lambda c: (0, c))),
        (expand, pl.BlockSpec((D, width), lambda c: (0, c))),
        (reduce, pl.BlockSpec((width, D), lambda c: (c, 0))),
    ]
    outs = [((tokens, D), F32)]
    if layout.direct:
        half = layout.devices // 2
        outs += [((half, layout.rows, 2 * FF + SMALL), BF16)] * 2
    else:
        outs += [((1, D, FF + SMALL), BF16), ((FF, D), BF16)]
    return pl.pallas_call(
        functools.partial(feed_back_kernel, layout, layer, back is not None),
        grid=(chunks,),
        in_specs=[pl.BlockSpec(memory_space=pltpu.SMEM), const(16, FF)] + [spec for _, spec in ins],
        out_specs=[const(*shape) for shape, _ in outs],
        out_shape=[jax.ShapeDtypeStruct(shape, kind) for shape, kind in outs],
        scratch_shapes=[
            pltpu.VMEM((tokens, D), BF16),
            pltpu.VMEM((tokens, D), BF16),
            pltpu.VMEM((tokens, D), F32),
            pltpu.VMEM((8, D), F32),
            pltpu.VMEM((1, FF), F32),
        ],
        compiler_params=pltpu.CompilerParams(vmem_limit_bytes=VMEM_BYTES),
        cost_estimate=pl.CostEstimate(
            flops=tokens * D * FF * 8, bytes_accessed=30 << 20, transcendentals=0
        ),
        name="feed_back",
    )(info, table, *[array for array, _ in ins])


def attend_back_kernel(g_first, queries, keys, values, soft, attended, qkv, merge, g_own, g_flank, g_packed, g_before, turned, turned_before):
    g_mixed = g_first[...].astype(BF16)
    g_attended = dot(merge[...], g_mixed, 1, 1)
    for head in range(HEADS):
        at = pl.ds(head * HEAD_DIM, HEAD_DIM)
        grad = g_attended[head * HEAD_DIM : (head + 1) * HEAD_DIM, :].astype(BF16)
        row_dot = jnp.sum(
            grad.astype(F32) * attended[at, :].astype(F32), axis=0, keepdims=True
        )
        low = soft[0, head]
        g_soft = dot(values[0, at, :], grad, 0, 0)
        g_scores = (low.astype(F32) * (g_soft - row_dot)).astype(BF16)
        g_values = dot(grad, low, 1, 1)
        g_keys = dot(queries[0, at, :], g_scores, 1, 1)
        turned[at, :] = dot(keys[0, at, :], g_scores, 1, 0) * HEAD_DIM ** (-0.5)
        turned[pl.ds(D + head * HEAD_DIM, HEAD_DIM), :] = g_keys[:, SPAN:]
        turned[pl.ds(2 * D + head * HEAD_DIM, HEAD_DIM), :] = g_values[:, SPAN:]
        turned_before[at, :] = g_keys[:, :SPAN]
        turned_before[pl.ds(D + head * HEAD_DIM, HEAD_DIM), :] = g_values[:, :SPAN]
    before = jnp.transpose(turned_before[...]).astype(BF16)
    g_before[...] = before
    g_flank[...] = dot(before, qkv[:, D:], 1, 1).astype(BF16)
    packed = jnp.transpose(turned[...]).astype(BF16)
    g_packed[...] = packed
    g_own[...] = g_first[...] + dot(packed, qkv[...], 1, 1)


def attend_back(g_first, queries, keys, values, soft, attended, qkv, merge):
    tokens = g_first.shape[0]
    canvases = tokens // SPAN
    const = lambda *shape: pl.BlockSpec(shape, lambda c: (0,) * len(shape))
    by_canvas = lambda *shape: pl.BlockSpec((1,) + shape, lambda c: (c,) + (0,) * len(shape))
    rows = lambda width: pl.BlockSpec((SPAN, width), lambda c: (c, 0))
    return pl.pallas_call(
        attend_back_kernel,
        grid=(canvases,),
        in_specs=[
            rows(D),
            by_canvas(D, SPAN),
            by_canvas(D, 2 * SPAN),
            by_canvas(D, 2 * SPAN),
            by_canvas(HEADS, 2 * SPAN, SPAN),
            pl.BlockSpec((D, SPAN), lambda c: (0, c)),
            const(D, 3 * D),
            const(D, D),
        ],
        out_specs=[rows(D), rows(D), rows(3 * D), rows(2 * D)],
        out_shape=[
            jax.ShapeDtypeStruct((tokens, D), F32),
            jax.ShapeDtypeStruct((tokens, D), BF16),
            jax.ShapeDtypeStruct((tokens, 3 * D), BF16),
            jax.ShapeDtypeStruct((tokens, 2 * D), BF16),
        ],
        scratch_shapes=[pltpu.VMEM((3 * D, SPAN), F32), pltpu.VMEM((2 * D, SPAN), F32)],
        compiler_params=pltpu.CompilerParams(vmem_limit_bytes=VMEM_BYTES),
        cost_estimate=pl.CostEstimate(
            flops=tokens * D * D * 2 * 20, bytes_accessed=20 << 20, transcendentals=0
        ),
        name="attend_back",
    )(g_first, queries, keys, values, soft, attended, qkv, merge)


def attend_weights_kernel(layout, info, hidden, flank, g_packed, g_before, attended, g_first, *targets):
    me = info[0]
    low = hidden[...].astype(BF16)
    store_blocks(me, dot(low, g_packed[:, :D], 0, 0).astype(BF16), targets, 0, layout)
    pair = dot(low, g_packed[:, D:], 0, 0) + dot(flank[...], g_before[...], 0, 0)
    store_blocks(me, pair.astype(BF16), targets, D, layout)
    mixed = dot(attended[...], g_first[...].astype(BF16), 1, 0)
    store_blocks(me, mixed.astype(BF16), targets, 3 * D, layout)


def attend_weights(layout, info, hidden, flank, g_packed, g_before, attended, g_first):
    if layout.direct:
        outs = [(layout.devices // 2, layout.rows, 4 * D)] * 2
    else:
        outs = [(1, D, 4 * D)]
    tokens = hidden.shape[0]
    return pl.pallas_call(
        functools.partial(attend_weights_kernel, layout),
        in_specs=[pl.BlockSpec(memory_space=pltpu.SMEM)]
        + [pl.BlockSpec(memory_space=pltpu.VMEM)] * 6,
        out_specs=[pl.BlockSpec(memory_space=pltpu.VMEM)] * len(outs),
        out_shape=[jax.ShapeDtypeStruct(shape, BF16) for shape in outs],
        compiler_params=pltpu.CompilerParams(vmem_limit_bytes=VMEM_BYTES),
        cost_estimate=pl.CostEstimate(
            flops=tokens * D * D * 2 * 6, bytes_accessed=12 << 20, transcendentals=0
        ),
        name="attend_weights",
    )(info, hidden, flank, g_packed, g_before, attended, g_first)


def shift_up(block, seq):
    return lax.ppermute(block, "seq", [(i, i + 1) for i in range(seq - 1)])


def shift_down(block, seq):
    return lax.ppermute(block, "seq", [(i + 1, i) for i in range(seq - 1)])


def shards(
    layout,
    canvas_input,
    crop_heights,
    qkv_weight,
    merge_weight,
    expand_weight,
    expand_bias,
    reduce_weight,
    reduce_bias,
    norm_gain,
    norm_shift,
    cotangent,
):
    seq, rows = layout.seq, layout.rows
    canvases, crops = crop_heights.shape
    tokens = canvases * SPAN
    seq_at = lax.axis_index("seq")
    me = (seq_at * layout.dp + lax.axis_index("dp")).astype(jnp.int32)
    kernel_me = me if layout.direct else me * 0
    first_row = (seq_at * BAND).astype(jnp.int32)
    info = jnp.concatenate(
        [kernel_me[None], first_row[None], crop_heights.reshape(-1).astype(jnp.int32)]
    )

    hidden = canvas_input.reshape(tokens, D)
    flank = shift_up(hidden, seq)

    small = jnp.concatenate(
        [
            expand_bias,
            reduce_bias,
            norm_gain[:, 0],
            norm_gain[:, 1],
            norm_shift[:, 0],
            norm_shift[:, 1],
        ],
        axis=1,
    )
    small = jnp.pad(small, ((0, rows - LAYERS), (0, SMALL - 9 * rows)))
    folded = (
        reduce_weight.reshape(LAYERS, 4, rows, D).transpose(0, 2, 1, 3).reshape(LAYERS, rows, 4 * D)
    )
    buffers = []
    for layer in range(LAYERS):
        parts = [qkv_weight[layer], merge_weight[layer]]
        if layer == 0:
            parts.append(small)
        parts += [expand_weight[layer], folded[layer]]
        buffers.append(gathered(jnp.concatenate(parts, axis=1), layout, me))

    table = None
    records = []
    for layer in range(LAYERS):
        arrays, codes = buffers[layer]
        if layer > 0:
            flank = shift_up(hidden, seq)
        held = attend(layout, layer == 0, info, hidden, flank, arrays, codes, crops)
        if layer == 0:
            qkv, merge, table, *rest = held
        else:
            qkv, merge, *rest = held
        queries, keys, values, soft, attended, first_in = rest
        lane = 4 * D + (SMALL if layer == 0 else 0)
        expand, reduce, second_in, lifted, slope, _, result_low = feed(
            layout, layer, info, table, first_in, arrays, codes, lane
        )
        records.append(
            (hidden, flank, qkv, merge, queries, keys, values, soft, attended, first_in, expand, reduce, second_in, lifted, slope)
        )
        hidden = result_low
    block_output = hidden.reshape(canvases, BAND, COLS, D)

    grad, back = cotangent.reshape(tokens, D), None
    pieces = [None] * LAYERS
    for layer in range(LAYERS - 1, -1, -1):
        (hidden, flank, qkv, merge, queries, keys, values, soft, attended, first_in, expand, reduce, second_in, lifted, slope) = records[layer]
        g_first, *feed_targets = feed_back(
            layout, layer, info, table, grad, back, second_in, first_in, lifted, slope, expand, reduce
        )
        if not layout.direct:
            both = feed_targets[0][0]
            turned = feed_targets[1].reshape(layout.devices, 4, rows, D).transpose(0, 2, 1, 3)
            feed_targets = [
                jnp.concatenate([both[:, :FF], turned.reshape(D, 4 * D), both[:, FF:]], axis=1)[None]
            ]
        g_own, g_flank, g_packed, g_before = attend_back(
            g_first, queries, keys, values, soft, attended, qkv, merge
        )
        back = shift_down(g_flank, seq)
        grad = g_own
        attend_targets = attend_weights(
            layout, info, hidden, flank, g_packed, g_before, attended, g_first
        )
        pieces[layer] = (
            scatter_sum(*split_blocks(feed_targets, layout, me), layout),
            scatter_sum(*split_blocks(attend_targets, layout, me), layout),
        )
    input_grad = (grad + back.astype(F32)).reshape(canvases, BAND, COLS, D)

    fed = jnp.stack([piece[0] for piece in pieces])
    met = jnp.stack([piece[1] for piece in pieces])
    vectors = fed[:, 0, 2 * FF :]
    part = lambda index, width: vectors[:, index * rows : index * rows + width]
    return (
        block_output,
        input_grad,
        met[:, :, : 3 * D],
        met[:, :, 3 * D :],
        fed[:, :, :FF],
        part(0, 4 * rows),
        fed[:, :, FF : 2 * FF].reshape(LAYERS, rows, 4, D).transpose(0, 2, 1, 3).reshape(LAYERS, 4 * rows, D),
        part(4, rows),
        jnp.stack([part(5, rows), part(6, rows)], axis=1),
        jnp.stack([part(7, rows), part(8, rows)], axis=1),
    )


def solution(mesh):
    layout = Layout(mesh.shape["seq"], mesh.shape["dp"])
    return jax.shard_map(
        functools.partial(shards, layout),
        mesh=mesh,
        in_specs=(
            P("dp", "seq", None, None),
            P("dp", None),
            P(None, ("seq", "dp"), None),
            P(None, ("seq", "dp"), None),
            P(None, ("seq", "dp"), None),
            P(None, ("seq", "dp")),
            P(None, ("seq", "dp"), None),
            P(None, ("seq", "dp")),
            P(None, None, ("seq", "dp")),
            P(None, None, ("seq", "dp")),
            P("dp", "seq", None, None),
        ),
        out_specs=(
            P("dp", "seq", None, None),
            P("dp", "seq", None, None),
            P(None, ("seq", "dp"), None),
            P(None, ("seq", "dp"), None),
            P(None, ("seq", "dp"), None),
            P(None, ("seq", "dp")),
            P(None, ("seq", "dp"), None),
            P(None, ("seq", "dp")),
            P(None, None, ("seq", "dp")),
            P(None, None, ("seq", "dp")),
        ),
        check_vma=False,
    )
```
